256 devices in a mesh: expert: 2 (over core), grp: 4 (over y), blk: 8 (over z_hi, x), head: 4 (over z_lo).
Axes of the slice: x: 4, y: 4, z: 8 (z_hi: 2, z_lo: 4; z = z_hi * 4 + z_lo), core: 2. Of those that a mesh axis runs over, the one named last changes fastest.
Arguments:
- queries: bfloat16 [2, 20480, 4096], P('expert', ('grp', 'blk', 'head')), parts along dimension 1, may hold values from -64 to 64
- keys: bfloat16 [2, 20480, 4096], P('expert', ('grp', 'blk', 'head')), parts along dimension 1, may hold values from -10 to 10
- values: bfloat16 [2, 20480, 4096], P('expert', ('grp', 'blk', 'head')), parts along dimension 1, may hold values from -6 to 6
- readout: bfloat16 [2, 4096, 64], P('expert'), may hold values from -0.375 to 0.375
- latents: float32 [128, 5120, 64], P('grp', ('blk', 'head')), parts along dimension 0, may hold values from -6 to 6
- valid: int32 [128], P('grp'), parts along dimension 0, may hold values from 2560 to 5120, as said below
- assignment: int32 [8], P('grp'), parts along dimension 0, may hold values from 0 to 31, as said below
- steps: int32 [8], P('grp'), parts along dimension 0, may hold values from 9 to 39, as said below
Outputs:
- attended: bfloat16 [2, 20480, 4096], P('expert', ('grp', 'blk', 'head')), parts along dimension 1
- next_latents: float32 [2, 20480, 64], P('expert', ('grp', 'blk', 'head')), parts along dimension 1
The draws below stay inside these ranges and needn't reach their ends.
There are 4 independent parts, one for each index of `grp`. The reference program is written for one: setup_inputs(seed, part) draws one part's arguments, and reference() takes and returns one part's arrays. A program takes and returns all parts, laid end to end along the dimension named above; an argument that names none is the same for every part. Nothing has to cross between parts.
Inputs may be any that keep to these rules, and one draw needn't show every extreme that they name: At least one queued clip has all 5120 tokens valid. `assignment`: two different clips, one of them the last queued clip 32 - 1; entry 0 goes to the high-noise expert, entry 1 to the low-noise one. `steps`: entry 0 is the last step before the switch to the low-noise expert; entry 1 is the sampler's last step, 39.
All inputs are finite; a program needn't handle non-finite values.
Results may differ from the reference program's by a relative error of at most 0.0065.
Values may be sent and summed in bfloat16 or wider, within the bound.
A program may use at most 256 MiB of HBM per device.

```python
import jax
import jax.numpy as jnp
from jax import lax

H = 32
HD = 128
PC = 64
STEPS = 40
CLIPS = 32
HW = 4096
TOKENS = 5120


def draw_queries(key, part):
    key = jax.random.fold_in(key, 1)
    drawn = 1.6 * jnp.clip(jax.random.normal(key, (2, TOKENS, HW), jnp.float32), -6.0, 6.0)
    return drawn.astype(jnp.bfloat16)


def draw_keys(key, part):
    key = jax.random.fold_in(key, 2)
    drawn = 1.6 * jnp.clip(jax.random.normal(key, (2, TOKENS, HW), jnp.float32), -6.0, 6.0)
    return drawn.astype(jnp.bfloat16)


def draw_values(key, part):
    key = jax.random.fold_in(key, 3)
    drawn = jnp.clip(jax.random.normal(key, (2, TOKENS, HW), jnp.float32), -6.0, 6.0)
    return drawn.astype(jnp.bfloat16)


def draw_valid(key, part):
    key = jax.random.fold_in(key, 5)
    counts = jax.random.randint(jax.random.fold_in(key, 1), (CLIPS,), TOKENS // 2, TOKENS + 1)
    full_clip = jax.random.randint(jax.random.fold_in(key, 2), (), 0, CLIPS)
    return jnp.where(jnp.arange(CLIPS) == full_clip, TOKENS, counts).astype(jnp.int32)


def draw_assignment(key, part):
    key = jax.random.fold_in(key, 6)
    other = jax.random.randint(jax.random.fold_in(key, 1), (), 0, CLIPS - 1)
    slot = jax.random.randint(jax.random.fold_in(key, 2), (), 0, 2)
    last = jnp.asarray(CLIPS - 1, jnp.int32)
    first_entry = jnp.where(slot == 0, last, other)
    second_entry = jnp.where(slot == 0, other, last)
    return jnp.stack([first_entry, second_entry]).astype(jnp.int32)


def draw_steps(key, part):
    key = jax.random.fold_in(key, 7)
    boundary = jax.random.randint(jax.random.fold_in(key, 1), (), 10, 31)
    return jnp.stack([boundary - 1, jnp.asarray(STEPS - 1, jnp.int32)]).astype(jnp.int32)


def block_scale(rng, dims, cuts, low, largest):
    level, own = 1.0, jax.random.fold_in(rng, 6)
    for axis_at, parts in cuts:
        steps = jnp.exp(jax.random.uniform(jax.random.fold_in(own, axis_at), (parts,), jnp.float32, low / len(cuts), largest / len(cuts)))
        level = level * jnp.repeat(steps, dims[axis_at] // parts).reshape([-1 if axis == axis_at else 1 for axis in range(len(dims))])
    return level


def noise(own_key, extent, width, reach, shards=(), kind=jnp.bfloat16):
    gain = block_scale(own_key, extent, shards, -0.22, 0.18) if shards else 1.0
    array = jax.random.normal(own_key, extent, jnp.float32) * width * gain
    return jnp.minimum(jnp.maximum(array, -reach), reach).astype(kind)


def setup_inputs(seed: int = 0, part: int = 0) -> dict:
    arg_keys = jax.random.split(jax.random.key(seed), 9)
    part_splits = jax.random.split(jax.random.fold_in(arg_keys[8], part), 9)
    return {
        "queries": draw_queries(jax.random.fold_in(jax.random.fold_in(arg_keys[8], part), 71), part),
        "keys": draw_keys(jax.random.fold_in(jax.random.fold_in(arg_keys[8], part), 71), part),
        "values": draw_values(jax.random.fold_in(jax.random.fold_in(arg_keys[8], part), 71), part),
        "readout": noise(arg_keys[3], (2, HW, PC), (HW // 16) ** -0.5, 0.375, ((0, 2),)),
        "latents": noise(part_splits[4], (CLIPS, TOKENS, PC), 1.0, 6.0, ((1, 32),), jnp.float32),
        "valid": draw_valid(jax.random.fold_in(jax.random.fold_in(arg_keys[8], part), 71), part),
        "assignment": draw_assignment(jax.random.fold_in(jax.random.fold_in(arg_keys[8], part), 71), part),
        "steps": draw_steps(jax.random.fold_in(jax.random.fold_in(arg_keys[8], part), 71), part),
    }


flow_shift = 5.0
masked_score = -1.0e30


def noise_level(step_value):
    fraction = 1.0 - step_value.astype(jnp.float32) / STEPS
    return flow_shift * fraction / (1.0 + (flow_shift - 1.0) * fraction)


def attend_clip(query_all, key_all, value_all, valid_count):
    def split_heads(matrix):
        return jnp.transpose(matrix.reshape(TOKENS, H, HD), (1, 0, 2)).astype(jnp.float32)

    positions = lax.iota(jnp.int32, TOKENS)
    usable = (positions < valid_count)[None, :]

    def one_head(triple):
        head_query, head_key, head_value = triple
        scores = jnp.dot(head_query, head_key.T, precision=lax.Precision.HIGHEST) * HD ** -0.5
        scores = jnp.where(usable, scores, masked_score)
        row_max = jnp.max(scores, axis=1, keepdims=True)
        weights = jnp.where(usable, jnp.exp(scores - row_max), 0.0)
        row_total = jnp.sum(weights, axis=1, keepdims=True)
        rounded = lax.optimization_barrier(weights.astype(jnp.bfloat16)).astype(jnp.float32)
        return jnp.dot(rounded, head_value, precision=lax.Precision.HIGHEST) / row_total

    outputs = lax.map(one_head, (split_heads(query_all), split_heads(key_all), split_heads(value_all)))
    outputs = jnp.transpose(outputs, (1, 0, 2)).reshape(TOKENS, H * HD)
    outputs = jnp.where((positions < valid_count)[:, None], outputs, 0.0)
    return outputs.astype(jnp.bfloat16)


def reference(queries, keys, values, readout, latents, valid, assignment, steps):
    attended_list = []
    advanced_list = []
    for section_index in range(2):
        clip_index = assignment[section_index]
        valid_count = valid[clip_index]
        attended = attend_clip(queries[section_index], keys[section_index], values[section_index], valid_count)
        velocity = jnp.dot(attended, readout[section_index], preferred_element_type=jnp.float32)
        step_value = steps[section_index]
        advanced = latents[clip_index] + (noise_level(step_value + 1) - noise_level(step_value)) * velocity
        attended_list.append(attended)
        advanced_list.append(advanced)
    return jnp.stack(attended_list), jnp.stack([advanced_list[1], advanced_list[0]])
```

```python
import functools

import jax
import jax.numpy as jnp
import numpy as np
from jax import lax
from jax.experimental import pallas as pl
from jax.experimental.pallas import tpu as pltpu
from jax.sharding import PartitionSpec as P

MESH = pl.DeviceIdType.MESH
HD = 128
PC = 64
STEPS = 40
FLOW_SHIFT = 5.0
MASKED = -1e30
SCORE_SCALE = float(HD**-0.5 / np.log(2.0))

ROWS = 160
XS, ZS, ZLO = 4, 8, 4
DEVICES = XS * ZS
TOKENS = DEVICES * ROWS
PAIRS = DEVICES // 2
BLOCK = 2 * ROWS
KEY_CHUNK = 1280
CHUNKS = TOKENS // KEY_CHUNK


def offset_of(step, side):
    dx, turn = step % 4, step // 4
    near = 3 - turn - turn // 2 + 2 * (turn // 3)
    if side == 0:
        return dx, near
    return (4 - dx) % 4, 8 - near - 4 * (1 - (near + 3) // 4)


def kernel(
    valid_ref, assignment_ref, steps_ref, q_ref, k_ref, v_ref, readout_ref, latents_ref,
    attended_ref, next_ref,
    k_in, k_two, v_two, q_in, o_out, o_in, bias, score_a, score_b, map_in, latents_in, handed_out, handed_in,
    k_send, k_recv, v_send, v_recv, q_send, q_recv, o_send, o_recv, own_sem, out_sem, hand_sem,
):
    expert, blk, head = lax.axis_index("expert"), lax.axis_index("blk"), lax.axis_index("head")
    my_x, my_z = blk % XS, (blk // XS) * ZLO + head
    me = blk * ZLO + head

    def partner(step, side, sign):
        dx, dz = offset_of(step, side)
        x = (my_x + sign * dx + XS) % XS
        z = (my_z + sign * dz + ZS) % ZS
        other_blk, other_head = (z // ZLO) * XS + x, z % ZLO
        return {"blk": other_blk, "head": other_head}, other_blk * ZLO + other_head

    own_step = 8

    def columns(index):
        return pl.ds(pl.multiple_of(index * HD, HD), HD)

    def rows(start, count):
        return pl.ds(pl.multiple_of(start, 32), count)

    def slot(step, side):
        return rows(step * BLOCK + side * ROWS, ROWS)

    def each_partner(action):
        def one(step, carry):
            @pl.when(step != own_step)
            def _():
                action(step, 0)

            action(step, 1)
            return carry

        lax.fori_loop(0, PAIRS, one, 0)

    barrier = pltpu.get_barrier_semaphore()
    swap = {"expert": 1 - expert}

    def greet(step, side):
        device, _ = partner(step, side, -1)
        pl.semaphore_signal(barrier, inc=1, device_id=device, device_id_type=MESH)

    each_partner(greet)
    pl.semaphore_signal(barrier, inc=1, device_id=swap, device_id_type=MESH)
    pl.semaphore_wait(barrier, DEVICES)

    def send_k(step, side):
        device, index = partner(step, side, 1)
        pltpu.make_async_remote_copy(
            k_ref.at[0, :, columns(index)], k_in.at[rows(me * ROWS, ROWS)], k_send, k_recv,
            device_id=device, device_id_type=MESH,
        ).start()

    def send_v(step, side):
        device, index = partner(step, side, 1)
        pltpu.make_async_remote_copy(
            v_ref.at[0, :, columns(index)], v_two.at[rows(me * ROWS, ROWS), pl.ds(0, HD)], v_send, v_recv,
            device_id=device, device_id_type=MESH,
        ).start()

    def send_q(step, side):
        device, index = partner(step, side, 1)
        pltpu.make_async_remote_copy(
            q_ref.at[0, :, columns(index)], q_in.at[slot(step, side)], q_send, q_recv.at[step],
            device_id=device, device_id_type=MESH,
        ).start()

    each_partner(send_k)
    own_k = pltpu.make_async_copy(k_ref.at[0, :, columns(me)], k_in.at[rows(me * ROWS, ROWS)], own_sem.at[0])
    own_k.start()
    own_v = pltpu.make_async_copy(
        v_ref.at[0, :, columns(me)], v_two.at[rows(me * ROWS, ROWS), pl.ds(0, HD)], own_sem.at[1]
    )
    own_v.start()
    own_q = pltpu.make_async_copy(q_ref.at[0, :, columns(me)], q_in.at[slot(own_step, 0)], own_sem.at[2])
    own_q.start()
    each_partner(send_v)
    each_partner(send_q)

    map_copy = pltpu.make_async_copy(readout_ref.at[0], map_in, own_sem.at[3])
    map_copy.start()
    latents_copy = pltpu.make_async_copy(latents_ref, latents_in, own_sem.at[4])
    latents_copy.start()

    clip = assignment_ref[expert]
    count = valid_ref[clip]
    v_two[:, HD:] = jnp.ones((TOKENS, HD), jnp.bfloat16)
    position = lax.broadcasted_iota(jnp.int32, (8, TOKENS), 1)
    bias[...] = jnp.where(position < count, 0.0, MASKED)

    own_k.wait()
    pltpu.make_async_copy(k_in.at[pl.ds(0, TOKENS - ROWS)], k_in.at[pl.ds(0, TOKENS - ROWS)], k_recv).wait()
    turned = jnp.transpose(k_in[...])
    k_two[0:HD, :] = turned
    k_two[HD:, :] = turned

    def queries_of(step):
        @pl.when(step != own_step)
        def _():
            pltpu.make_async_copy(q_in.at[rows(0, BLOCK)], q_in.at[rows(0, BLOCK)], q_recv.at[step]).wait()

        @pl.when(step == own_step)
        def _():
            own_q.wait()
            pltpu.make_async_copy(q_in.at[rows(0, ROWS)], q_in.at[rows(0, ROWS)], q_recv.at[step]).wait()

        scaled = q_in[rows(step * BLOCK, BLOCK), :].astype(jnp.float32) * SCORE_SCALE
        high = scaled.astype(jnp.bfloat16)
        low = (scaled - high.astype(jnp.float32)).astype(jnp.bfloat16)
        return jnp.concatenate([high, low], axis=1)

    def score_chunk(query, chunk, score_ref, most):
        at = slice(chunk * KEY_CHUNK, (chunk + 1) * KEY_CHUNK)
        scores = jnp.dot(query, k_two[:, at], preferred_element_type=jnp.float32)
        if (chunk + 1) * KEY_CHUNK > TOKENS // 2:
            scores = scores + bias[0:1, at]
        score_ref[:, at] = scores
        for lane in range(0, KEY_CHUNK, HD):
            piece = scores[:, lane : lane + HD]
            most = piece if most is None else jnp.maximum(most, piece)
        return most

    def value_chunk(top, chunk, score_ref, total):
        at = slice(chunk * KEY_CHUNK, (chunk + 1) * KEY_CHUNK)
        weights = jnp.exp2(score_ref[:, at] - top).astype(jnp.bfloat16)
        update = jnp.dot(weights, v_two[at, :], preferred_element_type=jnp.float32)
        return update if total is None else total + update

    def finish(step, total):
        outputs = total[:, :HD] / total[:, HD:]
        for side in range(2):
            device, index = partner(step, side, -1)
            token = index * ROWS + lax.broadcasted_iota(jnp.int32, (ROWS, HD), 0)
            kept = jnp.where(token < count, outputs[side * ROWS : (side + 1) * ROWS], 0.0)
            o_out[slot(step, side), :] = kept.astype(jnp.bfloat16)

            def send(device=device, side=side):
                pltpu.make_async_remote_copy(
                    o_out.at[slot(step, side)], o_in.at[slot(step, side)], o_send, o_recv.at[step],
                    device_id=device, device_id_type=MESH,
                ).start()

            if side == 0:
                pl.when(step != own_step)(send)
            else:
                send()

    def scored(step, score_ref):
        query, most = queries_of(step), None
        for chunk in range(CHUNKS):
            most = score_chunk(query, chunk, score_ref, most)
        return jnp.max(most, axis=1, keepdims=True)

    def turn(step, top, now_ref, next_ref):
        query = queries_of(step + 1)
        most = total = None
        for chunk in range(CHUNKS):
            most = score_chunk(query, chunk, next_ref, most)
            total = value_chunk(top, chunk, now_ref, total)
        finish(step, total)
        return jnp.max(most, axis=1, keepdims=True)

    top = scored(0, score_a)
    own_v.wait()
    pltpu.make_async_copy(k_in.at[pl.ds(0, TOKENS - ROWS)], k_in.at[pl.ds(0, TOKENS - ROWS)], v_recv).wait()

    def two_turns(half, top):
        top = turn(2 * half, top, score_a, score_b)
        return turn(2 * half + 1, top, score_b, score_a)

    top = lax.fori_loop(0, PAIRS // 2 - 1, two_turns, top)
    top = turn(PAIRS - 2, top, score_a, score_b)
    total = None
    for chunk in range(CHUNKS):
        total = value_chunk(top, chunk, score_b, total)
    finish(PAIRS - 1, total)

    def collect(step, velocity):
        @pl.when(step != own_step)
        def _():
            pltpu.make_async_copy(o_in.at[rows(0, BLOCK)], o_in.at[rows(0, BLOCK)], o_recv.at[step]).wait()

        @pl.when(step == own_step)
        def _():
            pltpu.make_async_copy(o_in.at[rows(0, ROWS)], o_in.at[rows(0, ROWS)], o_recv.at[step]).wait()
            o_in[slot(own_step, 0), :] = o_out[slot(own_step, 0), :]

        for side in range(2):
            _, index = partner(step, side, 1)
            pltpu.make_async_copy(
                o_in.at[slot(step, side)], attended_ref.at[0, :, columns(index)], out_sem
            ).start()
            velocity = velocity + lax.dot_general(
                map_in[:, columns(index)], o_in[slot(step, side), :], (((1,), (1,)), ((), ())),
                preferred_element_type=jnp.float32,
            )
        return velocity

    map_copy.wait()
    velocity = lax.fori_loop(0, PAIRS, collect, jnp.zeros((PC, ROWS), jnp.float32))

    def noise_level(step_value):
        fraction = 1.0 - step_value.astype(jnp.float32) / STEPS
        return FLOW_SHIFT * fraction / (1.0 + (FLOW_SHIFT - 1.0) * fraction)

    at = jnp.full((PC, ROWS), steps_ref[expert], jnp.int32)
    latents_copy.wait()
    handed_out[...] = latents_in[clip] + (noise_level(at + 1) - noise_level(at)) * velocity
    hand = pltpu.make_async_remote_copy(
        handed_out, handed_in, hand_sem.at[0], hand_sem.at[1], device_id=swap, device_id_type=MESH
    )
    hand.start()

    def sent(sem):
        pltpu.make_async_copy(k_in.at[pl.ds(0, TOKENS - ROWS)], k_in.at[pl.ds(0, TOKENS - ROWS)], sem).wait()

    sent(k_send)
    sent(v_send)
    sent(q_send)
    sent(o_send)
    pltpu.make_async_copy(o_in, o_in, out_sem).wait()
    hand.wait()
    next_ref[0] = handed_in[...]


def local(queries, keys, values, readout, latents, valid, assignment, steps):
    anywhere = pl.BlockSpec(memory_space=pl.ANY)
    scalars = pl.BlockSpec(memory_space=pltpu.SMEM)
    inside = pl.BlockSpec(memory_space=pltpu.VMEM)
    bf16, f32 = jnp.bfloat16, jnp.float32
    dma = pltpu.SemaphoreType.DMA
    readout, latents = jnp.swapaxes(readout, 1, 2), jnp.swapaxes(latents, 1, 2)
    attended, advanced = pl.pallas_call(
        kernel,
        out_shape=(
            jax.ShapeDtypeStruct((1, ROWS, DEVICES * HD), bf16),
            jax.ShapeDtypeStruct((1, PC, ROWS), f32),
        ),
        in_specs=[scalars, scalars, scalars, anywhere, anywhere, anywhere, anywhere, anywhere],
        out_specs=(anywhere, inside),
        scratch_shapes=[
            pltpu.VMEM((TOKENS, HD), bf16),
            pltpu.VMEM((2 * HD, TOKENS), bf16),
            pltpu.VMEM((TOKENS, 2 * HD), bf16),
            pltpu.VMEM((TOKENS, HD), bf16),
            pltpu.VMEM((TOKENS, HD), bf16),
            pltpu.VMEM((TOKENS, HD), bf16),
            pltpu.VMEM((8, TOKENS), f32),
            pltpu.VMEM((BLOCK, TOKENS), f32),
            pltpu.VMEM((BLOCK, TOKENS), f32),
            pltpu.VMEM((PC, DEVICES * HD), bf16),
            pltpu.VMEM(latents.shape, f32),
            pltpu.VMEM((PC, ROWS), f32),
            pltpu.VMEM((PC, ROWS), f32),
            dma, dma, dma, dma, dma, dma((PAIRS,)), dma, dma((PAIRS,)), dma((5,)), dma, dma((2,)),
        ],
        compiler_params=pltpu.CompilerParams(
            collective_id=0, has_side_effects=True, vmem_limit_bytes=56 * 2**20
        ),
    )(valid, assignment, steps, queries, keys, values, readout, latents)
    return attended, jnp.swapaxes(advanced, 1, 2)


def solution(mesh):
    tokens = P("expert", ("grp", "blk", "head"), None)
    return jax.shard_map(
        local,
        mesh=mesh,
        in_specs=(
            tokens, tokens, tokens,
            P("expert", None, None),
            P("grp", ("blk", "head"), None),
            P("grp"), P("grp"), P("grp"),
        ),
        out_specs=(tokens, tokens),
        check_vma=False,
    )
```

```python
import functools

import jax
import jax.numpy as jnp
import numpy as np
from jax import lax
from jax.experimental import pallas as pl
from jax.experimental.pallas import tpu as pltpu
from jax.sharding import PartitionSpec as P

MESH = pl.DeviceIdType.MESH
HD = 128
PC = 64
STEPS = 40
FLOW_SHIFT = 5.0
MASKED = -1e30
SCORE_SCALE = float(HD**-0.5 / np.log(2.0))

ROWS = 160
XS, ZS, ZLO = 4, 8, 4
DEVICES = XS * ZS
TOKENS = DEVICES * ROWS
PAIRS = DEVICES // 2
BLOCK = 2 * ROWS
KEY_CHUNK = 1280
CHUNKS = TOKENS // KEY_CHUNK


def offset_of(step, side):
    dx, turn = step % 4, step // 4
    near = 3 - turn - turn // 2 + 2 * (turn // 3)
    if side == 0:
        return dx, near
    return (4 - dx) % 4, 8 - near - 4 * (1 - (near + 3) // 4)


def kernel(
    valid_ref, assignment_ref, steps_ref, q_ref, k_ref, v_ref, readout_ref, latents_ref,
    attended_ref, advanced_ref,
    k_in, k_two, v_two, q_in, o_out, bias, score_a, score_b, map_in, latents_in,
    k_send, k_recv, v_send, v_recv, q_send, q_recv, o_send, o_recv, own_sem, relay_sem,
):
    expert, blk, head = lax.axis_index("expert"), lax.axis_index("blk"), lax.axis_index("head")
    my_x, my_z = blk % XS, (blk // XS) * ZLO + head
    me = blk * ZLO + head

    def partner(step, side, sign):
        dx, dz = offset_of(step, side)
        x = (my_x + sign * dx + XS) % XS
        z = (my_z + sign * dz + ZS) % ZS
        other_blk, other_head = (z // ZLO) * XS + x, z % ZLO
        return {"blk": other_blk, "head": other_head}, other_blk * ZLO + other_head

    own_step = 8

    def columns(index):
        return pl.ds(pl.multiple_of(index * HD, HD), HD)

    def rows(start, count):
        return pl.ds(pl.multiple_of(start, 32), count)

    def slot(step, side):
        return rows(step * BLOCK + side * ROWS, ROWS)

    def each_partner(action):
        def one(step, carry):
            @pl.when(step != own_step)
            def _():
                action(step, 0)

            action(step, 1)
            return carry

        lax.fori_loop(0, PAIRS, one, 0)

    def line_partners(action):
        def along_z(turn, carry):
            @pl.when(turn * 4 != own_step)
            def _():
                action(turn * 4, 0)

            action(turn * 4, 1)
            return carry

        def along_x(dx, carry):
            action(own_step + dx, 0)
            return carry

        lax.fori_loop(0, 4, along_z, 0)
        lax.fori_loop(1, XS, along_x, 0)

    def other_partners(action):
        def one(at, carry):
            step = (at // 3) * 4 + at % 3 + 1

            @pl.when(at // 3 != own_step // 4)
            def _():
                action(step, 0)

            action(step, 1)
            return carry

        lax.fori_loop(0, 12, one, 0)

    barrier = pltpu.get_barrier_semaphore()

    def greet(step, side):
        device, _ = partner(step, side, -1)
        pl.semaphore_signal(barrier, inc=1, device_id=device, device_id_type=MESH)

    line_partners(greet)
    pl.semaphore_wait(barrier, XS + ZS - 2)

    def send_k(step, side):
        device, index = partner(step, side, 1)
        pltpu.make_async_remote_copy(
            k_ref.at[0, :, columns(index)], k_in.at[rows(me * ROWS, ROWS)], k_send, k_recv,
            device_id=device, device_id_type=MESH,
        ).start()

    def send_v(step, side):
        device, index = partner(step, side, 1)
        pltpu.make_async_remote_copy(
            v_ref.at[0, :, columns(index)], v_two.at[rows(me * ROWS, ROWS), pl.ds(0, HD)], v_send, v_recv,
            device_id=device, device_id_type=MESH,
        ).start()

    def send_q(step, side):
        device, index = partner(step, side, 1)
        pltpu.make_async_remote_copy(
            q_ref.at[0, :, columns(index)], q_in.at[slot(step, side)], q_send, q_recv.at[step],
            device_id=device, device_id_type=MESH,
        ).start()

    line_partners(send_k)

    def relay(dx, carry):
        device, _ = partner(own_step + dx, 0, -1)
        pl.semaphore_signal(relay_sem, inc=1, device_id=device, device_id_type=MESH)
        return carry

    lax.fori_loop(1, XS, relay, 0)
    line_partners(send_v)
    pl.semaphore_wait(relay_sem, XS - 1)
    other_partners(send_k)
    own_k = pltpu.make_async_copy(k_ref.at[0, :, columns(me)], k_in.at[rows(me * ROWS, ROWS)], own_sem.at[0])
    own_k.start()
    own_v = pltpu.make_async_copy(
        v_ref.at[0, :, columns(me)], v_two.at[rows(me * ROWS, ROWS), pl.ds(0, HD)], own_sem.at[1]
    )
    own_v.start()
    own_q = pltpu.make_async_copy(q_ref.at[0, :, columns(me)], q_in.at[slot(own_step, 0)], own_sem.at[2])
    own_q.start()
    other_partners(send_v)
    each_partner(send_q)

    map_copy = pltpu.make_async_copy(readout_ref.at[0], map_in, own_sem.at[3])
    map_copy.start()
    latents_copy = pltpu.make_async_copy(latents_ref, latents_in, own_sem.at[4])
    latents_copy.start()

    clip = assignment_ref[expert]
    count = valid_ref[clip]
    v_two[:, HD:] = jnp.ones((TOKENS, HD), jnp.bfloat16)
    position = lax.broadcasted_iota(jnp.int32, (8, TOKENS), 1)
    bias[...] = jnp.where(position < count, 0.0, MASKED)

    own_k.wait()
    pltpu.make_async_copy(k_in.at[pl.ds(0, TOKENS - ROWS)], k_in.at[pl.ds(0, TOKENS - ROWS)], k_recv).wait()
    turned = jnp.transpose(k_in[...])
    k_two[0:HD, :] = turned
    k_two[HD:, :] = turned

    def queries_of(step):
        @pl.when(step != own_step)
        def _():
            pltpu.make_async_copy(q_in.at[rows(0, BLOCK)], q_in.at[rows(0, BLOCK)], q_recv.at[step]).wait()

        @pl.when(step == own_step)
        def _():
            own_q.wait()
            pltpu.make_async_copy(q_in.at[rows(0, ROWS)], q_in.at[rows(0, ROWS)], q_recv.at[step]).wait()

        scaled = q_in[rows(step * BLOCK, BLOCK), :].astype(jnp.float32) * SCORE_SCALE
        high = scaled.astype(jnp.bfloat16)
        low = (scaled - high.astype(jnp.float32)).astype(jnp.bfloat16)
        return jnp.concatenate([high, low], axis=1)

    def score_chunk(query, chunk, score_ref, most):
        at = slice(chunk * KEY_CHUNK, (chunk + 1) * KEY_CHUNK)
        scores = jnp.dot(query, k_two[:, at], preferred_element_type=jnp.float32)
        if (chunk + 1) * KEY_CHUNK > TOKENS // 2:
            scores = scores + bias[0:1, at]
        score_ref[:, at] = scores
        for lane in range(0, KEY_CHUNK, HD):
            piece = scores[:, lane : lane + HD]
            most = piece if most is None else jnp.maximum(most, piece)
        return most

    def value_chunk(top, chunk, score_ref, total):
        at = slice(chunk * KEY_CHUNK, (chunk + 1) * KEY_CHUNK)
        weights = jnp.exp2(score_ref[:, at] - top).astype(jnp.bfloat16)
        update = jnp.dot(weights, v_two[at, :], preferred_element_type=jnp.float32)
        return update if total is None else total + update

    def finish(step, total):
        outputs = total[:, :HD] / total[:, HD:]
        for side in range(2):
            device, index = partner(step, side, -1)
            token = index * ROWS + lax.broadcasted_iota(jnp.int32, (ROWS, HD), 0)
            kept = jnp.where(token < count, outputs[side * ROWS : (side + 1) * ROWS], 0.0)
            o_out[slot(step, side), :] = kept.astype(jnp.bfloat16)

            def send(device=device, side=side):
                pltpu.make_async_remote_copy(
                    o_out.at[slot(step, side)], attended_ref.at[0, :, columns(me)], o_send, o_recv.at[step],
                    device_id=device, device_id_type=MESH,
                ).start()

            if side == 0:
                pl.when(step != own_step)(send)
            else:
                send()

    def scored(step, score_ref):
        query, most = queries_of(step), None
        for chunk in range(CHUNKS):
            most = score_chunk(query, chunk, score_ref, most)
        return jnp.max(most, axis=1, keepdims=True)

    def turn(step, top, now_ref, next_ref):
        query = queries_of(step + 1)
        most = total = None
        for chunk in range(CHUNKS):
            most = score_chunk(query, chunk, next_ref, most)
            total = value_chunk(top, chunk, now_ref, total)
        finish(step, total)
        return jnp.max(most, axis=1, keepdims=True)

    top = scored(0, score_a)
    own_v.wait()
    pltpu.make_async_copy(k_in.at[pl.ds(0, TOKENS - ROWS)], k_in.at[pl.ds(0, TOKENS - ROWS)], v_recv).wait()

    def two_turns(half, top):
        top = turn(2 * half, top, score_a, score_b)
        return turn(2 * half + 1, top, score_b, score_a)

    top = lax.fori_loop(0, PAIRS // 2 - 1, two_turns, top)
    top = turn(PAIRS - 2, top, score_a, score_b)
    total = None
    for chunk in range(CHUNKS):
        total = value_chunk(top, chunk, score_b, total)
    finish(PAIRS - 1, total)

    def collect(step, velocity):
        @pl.when(step != own_step)
        def _():
            pltpu.make_async_copy(o_out.at[rows(0, BLOCK)], o_out.at[rows(0, BLOCK)], o_recv.at[step]).wait()

        @pl.when(step == own_step)
        def _():
            pltpu.make_async_copy(o_out.at[rows(0, ROWS)], o_out.at[rows(0, ROWS)], o_recv.at[step]).wait()
            attended_ref[0, :, columns(me)] = o_out[slot(own_step, 0), :]

        for side in range(2):
            _, index = partner(step, side, 1)
            velocity = velocity + lax.dot_general(
                map_in[:, columns(index)], attended_ref[0, :, columns(index)], (((1,), (1,)), ((), ())),
                preferred_element_type=jnp.float32,
            )
        return velocity

    map_copy.wait()
    velocity = lax.fori_loop(0, PAIRS, collect, jnp.zeros((PC, ROWS), jnp.float32))

    def noise_level(step_value):
        fraction = 1.0 - step_value.astype(jnp.float32) / STEPS
        return FLOW_SHIFT * fraction / (1.0 + (FLOW_SHIFT - 1.0) * fraction)

    at = jnp.full((PC, ROWS), steps_ref[expert], jnp.int32)
    latents_copy.wait()
    advanced_ref[0] = latents_in[clip] + (noise_level(at + 1) - noise_level(at)) * velocity

    def sent(sem):
        pltpu.make_async_copy(k_in.at[pl.ds(0, TOKENS - ROWS)], k_in.at[pl.ds(0, TOKENS - ROWS)], sem).wait()

    sent(k_send)
    sent(v_send)
    sent(q_send)
    sent(o_send)


def local(queries, keys, values, readout, latents, valid, assignment, steps):
    anywhere = pl.BlockSpec(memory_space=pl.ANY)
    scalars = pl.BlockSpec(memory_space=pltpu.SMEM)
    inside = pl.BlockSpec(memory_space=pltpu.VMEM)
    bf16, f32 = jnp.bfloat16, jnp.float32
    dma = pltpu.SemaphoreType.DMA
    readout, latents = jnp.swapaxes(readout, 1, 2), jnp.swapaxes(latents, 1, 2)
    attended, advanced = pl.pallas_call(
        kernel,
        out_shape=(
            pltpu.VMEM((1, ROWS, DEVICES * HD), bf16),
            pltpu.VMEM((1, PC, ROWS), f32),
        ),
        in_specs=[scalars, scalars, scalars, anywhere, anywhere, anywhere, anywhere, anywhere],
        out_specs=(inside, inside),
        scratch_shapes=[
            pltpu.VMEM((TOKENS, HD), bf16),
            pltpu.VMEM((2 * HD, TOKENS), bf16),
            pltpu.VMEM((TOKENS, 2 * HD), bf16),
            pltpu.VMEM((TOKENS, HD), bf16),
            pltpu.VMEM((TOKENS, HD), bf16),
            pltpu.VMEM((8, TOKENS), f32),
            pltpu.VMEM((BLOCK, TOKENS), f32),
            pltpu.VMEM((BLOCK, TOKENS), f32),
            pltpu.VMEM((PC, DEVICES * HD), bf16),
            pltpu.VMEM(latents.shape, f32),
            dma, dma, dma, dma, dma, dma((PAIRS,)), dma, dma((PAIRS,)), dma((5,)),
            pltpu.SemaphoreType.REGULAR,
        ],
        compiler_params=pltpu.CompilerParams(
            collective_id=0, has_side_effects=True, vmem_limit_bytes=56 * 2**20
        ),
    )(valid, assignment, steps, queries, keys, values, readout, latents)
    handed = lax.ppermute(advanced, "expert", [(0, 1), (1, 0)])
    return attended, jnp.swapaxes(handed, 1, 2)


def solution(mesh):
    tokens = P("expert", ("grp", "blk", "head"), None)
    return jax.shard_map(
        local,
        mesh=mesh,
        in_specs=(
            tokens, tokens, tokens,
            P("expert", None, None),
            P("grp", ("blk", "head"), None),
            P("grp"), P("grp"), P("grp"),
        ),
        out_specs=(tokens, tokens),
        check_vma=False,
    )
```

```python
import functools

import jax
import jax.numpy as jnp
import numpy as np
from jax import lax
from jax.experimental import pallas as pl
from jax.experimental.pallas import tpu as pltpu
from jax.sharding import PartitionSpec as P

MESH = pl.DeviceIdType.MESH
HD = 128
PC = 64
STEPS = 40
FLOW_SHIFT = 5.0
MASKED = -1e30
SCORE_SCALE = float(HD**-0.5 / np.log(2.0))

ROWS = 160
XS, ZS, ZLO = 4, 8, 4
DEVICES = XS * ZS
TOKENS = DEVICES * ROWS
PAIRS = DEVICES // 2
BLOCK = 2 * ROWS
KEY_CHUNK = 1280
CHUNKS = TOKENS // KEY_CHUNK


def offset_of(step, side):
    dx, turn = step % 4, step // 4
    near = (turn + 1) % 4
    if side == 0:
        return dx, near
    return (4 - dx) % 4, 8 - near - 4 * (1 - (near + 3) // 4)


def kernel(
    valid_ref, assignment_ref, steps_ref, q_ref, k_ref, v_ref, readout_ref, latents_ref,
    attended_ref, advanced_ref,
    k_in, k_two, v_two, q_in, o_out, bias, score_a, score_b, map_in, latents_in,
    k_send, k_recv, v_send, v_recv, q_send, q_recv, o_send, o_recv, own_sem, relay_sem,
):
    expert, blk, head = lax.axis_index("expert"), lax.axis_index("blk"), lax.axis_index("head")
    my_x, my_z = blk % XS, (blk // XS) * ZLO + head
    me = blk * ZLO + head

    def partner(step, side, sign):
        dx, dz = offset_of(step, side)
        x = (my_x + sign * dx + XS) % XS
        z = (my_z + sign * dz + ZS) % ZS
        other_blk, other_head = (z // ZLO) * XS + x, z % ZLO
        return {"blk": other_blk, "head": other_head}, other_blk * ZLO + other_head

    own_step = 12

    def columns(index):
        return pl.ds(pl.multiple_of(index * HD, HD), HD)

    def rows(start, count):
        return pl.ds(pl.multiple_of(start, 32), count)

    def slot(step, side):
        return rows(step * BLOCK + side * ROWS, ROWS)

    def each_partner(action):
        def one(step, carry):
            @pl.when(step != own_step)
            def _():
                action(step, 0)

            action(step, 1)
            return carry

        lax.fori_loop(0, PAIRS, one, 0)

    def line_partners(action):
        def along_z(turn, carry):
            @pl.when(turn * 4 != own_step)
            def _():
                action(turn * 4, 0)

            action(turn * 4, 1)
            return carry

        def along_x(dx, carry):
            action(own_step + dx, 0)
            return carry

        lax.fori_loop(0, 4, along_z, 0)
        lax.fori_loop(1, XS, along_x, 0)

    def other_partners(action):
        def one(at, carry):
            step = (at // 3) * 4 + at % 3 + 1

            @pl.when(at // 3 != own_step // 4)
            def _():
                action(step, 0)

            action(step, 1)
            return carry

        lax.fori_loop(0, 12, one, 0)

    barrier = pltpu.get_barrier_semaphore()

    def greet(step, side):
        device, _ = partner(step, side, -1)
        pl.semaphore_signal(barrier, inc=1, device_id=device, device_id_type=MESH)

    line_partners(greet)
    pl.semaphore_wait(barrier, XS + ZS - 2)

    def send_k(step, side):
        device, index = partner(step, side, 1)
        pltpu.make_async_remote_copy(
            k_ref.at[0, :, columns(index)], k_in.at[rows(me * ROWS, ROWS)], k_send, k_recv,
            device_id=device, device_id_type=MESH,
        ).start()

    def send_v(step, side):
        device, index = partner(step, side, 1)
        pltpu.make_async_remote_copy(
            v_ref.at[0, :, columns(index)], v_two.at[rows(me * ROWS, ROWS), pl.ds(0, HD)], v_send, v_recv,
            device_id=device, device_id_type=MESH,
        ).start()

    def send_q(step, side):
        device, index = partner(step, side, 1)
        pltpu.make_async_remote_copy(
            q_ref.at[0, :, columns(index)], q_in.at[slot(step, side)], q_send, q_recv.at[step],
            device_id=device, device_id_type=MESH,
        ).start()

    line_partners(send_k)

    def relay(dx, carry):
        device, _ = partner(own_step + dx, 0, -1)
        pl.semaphore_signal(relay_sem, inc=1, device_id=device, device_id_type=MESH)
        return carry

    lax.fori_loop(1, XS, relay, 0)
    line_partners(send_v)
    pl.semaphore_wait(relay_sem, XS - 1)
    other_partners(send_k)
    own_k = pltpu.make_async_copy(k_ref.at[0, :, columns(me)], k_in.at[rows(me * ROWS, ROWS)], own_sem.at[0])
    own_k.start()
    own_v = pltpu.make_async_copy(
        v_ref.at[0, :, columns(me)], v_two.at[rows(me * ROWS, ROWS), pl.ds(0, HD)], own_sem.at[1]
    )
    own_v.start()
    own_q = pltpu.make_async_copy(q_ref.at[0, :, columns(me)], q_in.at[slot(own_step, 0)], own_sem.at[2])
    own_q.start()
    other_partners(send_v)
    each_partner(send_q)

    map_copy = pltpu.make_async_copy(readout_ref.at[0], map_in, own_sem.at[3])
    map_copy.start()
    latents_copy = pltpu.make_async_copy(latents_ref, latents_in, own_sem.at[4])
    latents_copy.start()

    clip = assignment_ref[expert]
    count = valid_ref[clip]
    v_two[:, HD:] = jnp.ones((TOKENS, HD), jnp.bfloat16)
    position = lax.broadcasted_iota(jnp.int32, (8, TOKENS), 1)
    bias[...] = jnp.where(position < count, 0.0, MASKED)

    own_k.wait()
    pltpu.make_async_copy(k_in.at[pl.ds(0, TOKENS - ROWS)], k_in.at[pl.ds(0, TOKENS - ROWS)], k_recv).wait()
    turned = jnp.transpose(k_in[...])
    k_two[0:HD, :] = turned
    k_two[HD:, :] = turned

    def queries_of(step):
        @pl.when(step != own_step)
        def _():
            pltpu.make_async_copy(q_in.at[rows(0, BLOCK)], q_in.at[rows(0, BLOCK)], q_recv.at[step]).wait()

        @pl.when(step == own_step)
        def _():
            own_q.wait()
            pltpu.make_async_copy(q_in.at[rows(0, ROWS)], q_in.at[rows(0, ROWS)], q_recv.at[step]).wait()

        scaled = q_in[rows(step * BLOCK, BLOCK), :].astype(jnp.float32) * SCORE_SCALE
        high = scaled.astype(jnp.bfloat16)
        low = (scaled - high.astype(jnp.float32)).astype(jnp.bfloat16)
        return jnp.concatenate([high, low], axis=1)

    def score_chunk(query, chunk, score_ref, most):
        at = slice(chunk * KEY_CHUNK, (chunk + 1) * KEY_CHUNK)
        scores = jnp.dot(query, k_two[:, at], preferred_element_type=jnp.float32)
        if (chunk + 1) * KEY_CHUNK > TOKENS // 2:
            scores = scores + bias[0:1, at]
        score_ref[:, at] = scores
        for lane in range(0, KEY_CHUNK, HD):
            piece = scores[:, lane : lane + HD]
            most = piece if most is None else jnp.maximum(most, piece)
        return most

    def value_chunk(top, chunk, score_ref, total):
        at = slice(chunk * KEY_CHUNK, (chunk + 1) * KEY_CHUNK)
        weights = jnp.exp2(score_ref[:, at] - top).astype(jnp.bfloat16)
        update = jnp.dot(weights, v_two[at, :], preferred_element_type=jnp.float32)
        return update if total is None else total + update

    def finish(step, total):
        outputs = total[:, :HD] / total[:, HD:]
        for side in range(2):
            device, index = partner(step, side, -1)
            token = index * ROWS + lax.broadcasted_iota(jnp.int32, (ROWS, HD), 0)
            kept = jnp.where(token < count, outputs[side * ROWS : (side + 1) * ROWS], 0.0)
            o_out[slot(step, side), :] = kept.astype(jnp.bfloat16)

            def send(device=device, side=side):
                pltpu.make_async_remote_copy(
                    o_out.at[slot(step, side)], attended_ref.at[0, :, columns(me)], o_send, o_recv.at[step],
                    device_id=device, device_id_type=MESH,
                ).start()

            if side == 0:
                pl.when(step != own_step)(send)
            else:
                send()

    def scored(step, score_ref):
        query, most = queries_of(step), None
        for chunk in range(CHUNKS):
            most = score_chunk(query, chunk, score_ref, most)
        return jnp.max(most, axis=1, keepdims=True)

    def turn(step, top, now_ref, next_ref):
        query = queries_of(step + 1)
        most = total = None
        for chunk in range(CHUNKS):
            most = score_chunk(query, chunk, next_ref, most)
            total = value_chunk(top, chunk, now_ref, total)
        finish(step, total)
        return jnp.max(most, axis=1, keepdims=True)

    top = scored(0, score_a)
    own_v.wait()
    pltpu.make_async_copy(k_in.at[pl.ds(0, TOKENS - ROWS)], k_in.at[pl.ds(0, TOKENS - ROWS)], v_recv).wait()

    def two_turns(half, top):
        top = turn(2 * half, top, score_a, score_b)
        return turn(2 * half + 1, top, score_b, score_a)

    top = lax.fori_loop(0, PAIRS // 2 - 1, two_turns, top)
    top = turn(PAIRS - 2, top, score_a, score_b)
    total = None
    for chunk in range(CHUNKS):
        total = value_chunk(top, chunk, score_b, total)
    finish(PAIRS - 1, total)

    def collect(step, velocity):
        @pl.when(step != own_step)
        def _():
            pltpu.make_async_copy(o_out.at[rows(0, BLOCK)], o_out.at[rows(0, BLOCK)], o_recv.at[step]).wait()

        @pl.when(step == own_step)
        def _():
            pltpu.make_async_copy(o_out.at[rows(0, ROWS)], o_out.at[rows(0, ROWS)], o_recv.at[step]).wait()
            attended_ref[0, :, columns(me)] = o_out[slot(own_step, 0), :]

        for side in range(2):
            _, index = partner(step, side, 1)
            velocity = velocity + lax.dot_general(
                map_in[:, columns(index)], attended_ref[0, :, columns(index)], (((1,), (1,)), ((), ())),
                preferred_element_type=jnp.float32,
            )
        return velocity

    map_copy.wait()
    velocity = lax.fori_loop(0, PAIRS, collect, jnp.zeros((PC, ROWS), jnp.float32))

    def noise_level(step_value):
        fraction = 1.0 - step_value.astype(jnp.float32) / STEPS
        return FLOW_SHIFT * fraction / (1.0 + (FLOW_SHIFT - 1.0) * fraction)

    at = jnp.full((PC, ROWS), steps_ref[expert], jnp.int32)
    latents_copy.wait()
    advanced_ref[0] = latents_in[clip] + (noise_level(at + 1) - noise_level(at)) * velocity

    def sent(sem):
        pltpu.make_async_copy(k_in.at[pl.ds(0, TOKENS - ROWS)], k_in.at[pl.ds(0, TOKENS - ROWS)], sem).wait()

    sent(k_send)
    sent(v_send)
    sent(q_send)
    sent(o_send)


def local(queries, keys, values, readout, latents, valid, assignment, steps):
    anywhere = pl.BlockSpec(memory_space=pl.ANY)
    scalars = pl.BlockSpec(memory_space=pltpu.SMEM)
    inside = pl.BlockSpec(memory_space=pltpu.VMEM)
    bf16, f32 = jnp.bfloat16, jnp.float32
    dma = pltpu.SemaphoreType.DMA
    readout, latents = jnp.swapaxes(readout, 1, 2), jnp.swapaxes(latents, 1, 2)
    attended, advanced = pl.pallas_call(
        kernel,
        out_shape=(
            pltpu.VMEM((1, ROWS, DEVICES * HD), bf16),
            pltpu.VMEM((1, PC, ROWS), f32),
        ),
        in_specs=[scalars, scalars, scalars, anywhere, anywhere, anywhere, anywhere, anywhere],
        out_specs=(inside, inside),
        scratch_shapes=[
            pltpu.VMEM((TOKENS, HD), bf16),
            pltpu.VMEM((2 * HD, TOKENS), bf16),
            pltpu.VMEM((TOKENS, 2 * HD), bf16),
            pltpu.VMEM((TOKENS, HD), bf16),
            pltpu.VMEM((TOKENS, HD), bf16),
            pltpu.VMEM((8, TOKENS), f32),
            pltpu.VMEM((BLOCK, TOKENS), f32),
            pltpu.VMEM((BLOCK, TOKENS), f32),
            pltpu.VMEM((PC, DEVICES * HD), bf16),
            pltpu.VMEM(latents.shape, f32),
            dma, dma, dma, dma, dma, dma((PAIRS,)), dma, dma((PAIRS,)), dma((5,)),
            pltpu.SemaphoreType.REGULAR,
        ],
        compiler_params=pltpu.CompilerParams(
            collective_id=0, has_side_effects=True, vmem_limit_bytes=56 * 2**20
        ),
    )(valid, assignment, steps, queries, keys, values, readout, latents)
    handed = lax.ppermute(advanced, "expert", [(0, 1), (1, 0)])
    return attended, jnp.swapaxes(handed, 1, 2)


def solution(mesh):
    tokens = P("expert", ("grp", "blk", "head"), None)
    return jax.shard_map(
        local,
        mesh=mesh,
        in_specs=(
            tokens, tokens, tokens,
            P("expert", None, None),
            P("grp", ("blk", "head"), None),
            P("grp"), P("grp"), P("grp"),
        ),
        out_specs=(tokens, tokens),
        check_vma=False,
    )
```
